32 devices in a mesh: groups: 2 (over x), store: 4 (over y, core), tensor: 4 (over z).
Axes of the slice: x: 2, y: 2, z: 4, core: 2. Of those that a mesh axis runs over, the one named last changes fastest.
Arguments:
- queries: bfloat16 [16384, 4096], P(('groups', 'store'), 'tensor'), parts along dimension 0, may hold values from -6 to 6
- suffix_cache: bfloat16 [16384, 2, 1024], P(('groups', 'store'), None, 'tensor'), parts along dimension 0, may hold values from -5 to 5
- cache_blocks: bfloat16 [128, 2, 128, 1024], P(('groups', 'store'), None, None, 'tensor'), parts along dimension 0, may hold values from -6 to 6
- cache_states: bfloat16 [32, 4096, 128], P(('groups', 'store'), 'tensor'), parts along dimension 0, may hold values from -5 to 5
- ssm_input: bfloat16 [16384, 4096], P(('groups', 'store'), 'tensor'), parts along dimension 0, may hold values from -60 to 60
- gate_input: bfloat16 [16384, 4096], P(('groups', 'store'), 'tensor'), parts along dimension 0, may hold values from -5 to 5
- state_maps: bfloat16 [16384, 2, 128], P(('groups', 'store')), parts along dimension 0, may hold values from -1.5 to 1.5
- step_size: float32 [128, 8192], P(('groups', 'tensor'), 'store'), parts along dimension 0, may hold values from 0 to 0.4
- decay_log: float32 [64], P('tensor'), may hold values from -0.5 to 0.5
- skip: float32 [64], P('tensor'), may hold values from 0.5 to 12
- norm_gain: float32 [4096], P('tensor'), may hold values from 0.1 to 1.9
- hit_owner: int32 [32, 8, 1], P('groups'), parts along dimension 0, may hold values from 0 to 3; in each aligned block of 32 rows (0 to 31, 32 to 63, ..., all dimensions but the last counted through in order) at most 16 rows name the same one
- hit_block: int32 [32, 8], P('groups'), parts along dimension 0, may hold values from 0 to 15
- hit_len: int32 [32], P('groups'), parts along dimension 0, may hold values from 1 to 8, 112 in all
- saved_owner: int32 [32, 1], P('groups'), parts along dimension 0, may hold values from 0 to 3; in each aligned block of 4 rows (0 to 3, 4 to 7, ...) at most 2 rows name the same one
- saved_slot: int32 [32], P('groups'), parts along dimension 0, may hold values from 0 to 3
Outputs:
- attn_out: bfloat16 [16384, 4096], P(('groups', 'store'), 'tensor'), parts along dimension 0
- ssm_out: bfloat16 [16384, 4096], P(('groups', 'store'), 'tensor'), parts along dimension 0
- final_state: float32 [32, 4096, 128], P(('groups', 'store'), 'tensor'), parts along dimension 0
The draws below stay inside these ranges and needn't reach their ends.
There are 2 independent parts, one for each index of `groups`. The reference program is written for one: setup_inputs(seed, part) draws one part's arguments, and reference() takes and returns one part's arrays. A program takes and returns all parts, laid end to end along the dimension named above; an argument that names none is the same for every part. Nothing has to cross between parts.
Inputs may be any that keep to these rules, and one draw needn't show every extreme that they name: `hit_owner`: among the 32 entries of the 4 requests of one store index, no owner is named more than 16 times, a bound that some block reaches. `hit_len`: the longest match is exactly 8 blocks. `saved_owner`: among the 4 requests of one store index, no owner holds more than 2 of their checkpoints, a bound that some block reaches.
All inputs are finite; a program needn't handle non-finite values.
Results may differ from the reference program's by a relative error of at most 0.0046.
Values may be sent and summed in bfloat16 or wider, within the bound.
A program may use at most 128 MiB of HBM per device.

```python
import math
import jax
import jax.numpy as jnp
import numpy as np
from jax import lax

HEADS = 32
ATTENDED_GROUPS = 8
HEAD_DIM = 128
SSM_HEADS = 64
SSM_DIM = 64
STATE = 128
BLOCK = 128
STRETCH = 128
MAX_BLOCKS = 8
REQUEST_NEW = 512
REQ_DEV = 4
POOL = 16
SAVED = 4
REQS = 16
ALL_NEW_ENTRIES = 8192
POOLS = 64
SAVED_ALL = 16
SLOTS = 16
STATE_SLOTS = 2
N_STORE = 4


def draw_cache_blocks(key, part):
    key = jax.random.fold_in(key, 11)
    shape = (POOLS, 2, BLOCK, ATTENDED_GROUPS * HEAD_DIM)
    base = jax.random.truncated_normal(key, -5.0, 5.0, shape, jnp.float32)
    return base.astype(jnp.bfloat16)


def draw_queries(key, part):
    key = jax.random.fold_in(key, 12)
    shape = (ALL_NEW_ENTRIES, HEADS * HEAD_DIM)
    base = jax.random.truncated_normal(key, -5.0, 5.0, shape, jnp.float32)
    return base.astype(jnp.bfloat16)


def draw_step_size(key, part):
    key = jax.random.fold_in(key, 13)
    first, second, third, fourth, quintile_share = jax.random.split(key, 5)
    quick = jax.random.randint(first, (SSM_HEADS, 1), 0, 2) == 0
    slow_level = jnp.exp(jax.random.uniform(second, (SSM_HEADS, 1), jnp.float32, math.log(0.1 / REQUEST_NEW), math.log(1.0 / REQUEST_NEW)))
    quick_level = jnp.exp(jax.random.uniform(third, (SSM_HEADS, 1), jnp.float32, math.log(0.02), math.log(0.04)))
    quantize_factor = jnp.where(quick, quick_level, slow_level)
    approximate_output = jax.random.uniform(fourth, (SSM_HEADS, ALL_NEW_ENTRIES), jnp.float32, 0.5, 1.5)
    grouped_lines = jax.random.randint(quintile_share, (1, ALL_NEW_ENTRIES), 0, max(REQUEST_NEW // 2, 2)) == 0
    return (quantize_factor * approximate_output + jnp.where(grouped_lines, 0.3, 0.0)).astype(jnp.float32)


def draw_skip(key, part):
    key = jax.random.fold_in(key, 14)
    place = jnp.arange(SSM_HEADS).astype(jnp.float32) / (SSM_HEADS - 1)
    factor = jax.random.uniform(key, (SSM_HEADS,), jnp.float32, 0.6, 1.4)
    return (jnp.exp(math.log(3.0) * place) * factor).astype(jnp.float32)


def draw_ssm_input(key, part):
    key = jax.random.fold_in(key, 15)
    first, second, third = jax.random.split(key, 3)
    width = SSM_HEADS * SSM_DIM
    row_scale = jnp.exp(jax.random.uniform(first, (ALL_NEW_ENTRIES, 1), jnp.float32, 0.0, math.log(10.0))) / 3.0
    column_scale = jnp.exp(jax.random.uniform(second, (1, width), jnp.float32, 0.0, math.log(10.0))) / 3.0
    base = jax.random.truncated_normal(third, -5.0, 5.0, (ALL_NEW_ENTRIES, width), jnp.float32)
    return (base * row_scale * column_scale).astype(jnp.bfloat16)


def set_ends(array, own_key, low, high):
    dims = array.shape
    spot = [jax.random.randint(jax.random.fold_in(own_key, axis), (), 0, dims[axis]) for axis in range(len(dims))]
    array = array.at[tuple(spot)].set(low)
    longest = dims.index(max(dims))
    spot[longest] = (spot[longest] + 1) % dims[longest]
    return array.at[tuple(spot)].set(high)


def block_levels(own_key, extent, shards, low, largest):
    def one(dim, shards_of):
        heights = jax.random.uniform(jax.random.fold_in(jax.random.fold_in(own_key, 6), dim), (shards_of,), jnp.float32, low / len(shards), largest / len(shards))
        return jnp.repeat(jnp.exp(heights), extent[dim] // shards_of).reshape((-1,) + (1,) * (len(extent) - dim - 1))

    loudness = one(*shards[0])
    for cut in shards[1:]:
        loudness = loudness * one(*cut)
    return loudness


def split_up(count, total, bound, lean):
    weights = [(1 << 20) // math.isqrt(standing ** lean) + 1 for standing in range(2, count + 1)]
    rest, holding = total - bound - (count - 1), [1] * (count - 1)
    while rest > 0:
        candidates = [i for i in range(count - 1) if holding[i] < bound]
        whole, budget = sum([weights[i] for i in candidates]), rest
        for i in candidates:
            more = min(bound - holding[i], max(1, budget * weights[i] // whole), rest)
            holding[i] = holding[i] + more
            rest = rest - more
    return np.array([bound] + holding)


def ragged_sizes(own_key, number_of, total, bound, lean):
    if number_of == 2:
        one = jax.random.randint(own_key, (), max(1, total - bound), min(bound, total - 1) + 1)
        return jnp.stack([one, total - one])
    sizes = jnp.asarray(split_up(number_of, total, bound, lean), jnp.int32)
    couples = (number_of - 1) // 2
    giver, taker = sizes[1:1 + 2 * couples:2], sizes[2:2 + 2 * couples:2]
    margin = jnp.minimum(giver - 1, bound - taker)
    moved = jax.random.randint(jax.random.fold_in(own_key, 1), (couples,), 0, 1 << 20) % (margin + 1)
    sizes = sizes.at[1:1 + 2 * couples:2].set(giver - moved).at[2:2 + 2 * couples:2].set(taker + moved)
    return sizes[jax.random.permutation(jax.random.fold_in(own_key, 2), number_of)]


def deal_out(stream_key, own, number, rows, count, top, most, skew):
    ranking = jax.random.permutation(stream_key, count)
    crowded, ordinary = portions_of(count, rows * top, most, skew, True), portions_of(count, rows * top, most, skew, False)
    places = jnp.arange(count)

    def named(lengths, turn):
        used = int((lengths > 0).sum())
        fixed = max(1, used // 4)
        shifted = fixed + (places - fixed + turn * (used - fixed)) % max(1, count - fixed)
        return jnp.zeros((count,), jnp.int32).at[ranking[jnp.where(places < fixed, places, shifted)]].set(jnp.asarray(lengths, jnp.int32))

    lengths = jnp.where(number % 4 == 0, named(crowded, number // 4), named(ordinary, number - number // 4 - 1))
    mixed = jax.random.permutation(jax.random.fold_in(own, 3), count)
    giver, receiver = mixed[0:count // 2 * 2:2], mixed[1:count // 2 * 2:2]
    margin = jnp.minimum(lengths[giver] - 1, most - lengths[receiver]) // 2
    margin = jnp.where((giver == ranking[0]) | (receiver == ranking[0]) | (lengths[receiver] == 0), 0, jnp.maximum(margin, 0))
    shifted = jax.random.randint(jax.random.fold_in(own, 4), (count // 2,), 0, 1 << 20) % (margin + 1)
    lengths = lengths.at[giver].add(-shifted).at[receiver].add(shifted)
    items = jnp.searchsorted(jnp.cumsum(lengths), jnp.arange(rows * top), side="right").astype(jnp.int32)
    grid = items.reshape(top, rows).T
    grid = grid[jax.random.permutation(jax.random.fold_in(own, 1), rows)]
    turn = jax.random.randint(jax.random.fold_in(own, 2), (rows, 1), 0, top)
    return jnp.take_along_axis(grid, (jnp.arange(top)[None, :] + turn) % top, axis=1)


def portions_of(amount, total, limit, lean, full):
    weights = [(1 << 20) // math.isqrt(standing ** lean) + 1 for standing in range(1, amount + 1)]
    largest = limit if full else min(limit, max(-(-total // amount), total * weights[0] // sum(weights)))
    least = 1 if total - largest >= amount - 1 else 0
    holding, surplus = [largest] + [least] * (amount - 1), total - largest - least * (amount - 1)
    while surplus > 0:
        movable = [i for i in range(1, amount) if holding[i] < largest] or [i for i in range(1, amount) if holding[i] < limit]
        pool, left = sum([weights[i] for i in movable]), surplus
        for i in movable:
            more = min(limit - holding[i], max(1, left * weights[i] // pool), surplus)
            holding[i] = holding[i] + more
            surplus = surplus - more
    return np.array(holding)


def gaussian(own_key, shape, deviation, most, cuts=(), kind=jnp.bfloat16):
    array = jax.random.normal(own_key, shape, jnp.float32) * deviation
    if len(cuts) > 0:
        array = block_levels(own_key, shape, cuts, -0.22, 0.18) * array
    return jnp.clip(array, min=-most, max=most).astype(kind)


def setup_inputs(seed: int = 0, part: int = 0) -> dict:
    key_list = jax.random.split(jax.random.key(seed), 17)
    part_splits = jax.random.split(jax.random.fold_in(key_list[16], part), 17)
    queries = draw_queries(jax.random.fold_in(jax.random.fold_in(key_list[16], part), 71), part)
    suffix_cache = gaussian(part_splits[1], (ALL_NEW_ENTRIES, 2, ATTENDED_GROUPS * HEAD_DIM), 1.0, 5.0, ((0, 4), (2, 4)))
    cache_blocks = draw_cache_blocks(jax.random.fold_in(jax.random.fold_in(key_list[16], part), 71), part)
    cache_states = gaussian(part_splits[3], (SAVED_ALL, SSM_HEADS * SSM_DIM, STATE), 1.0, 5.0, ((0, 4), (1, 4)))
    ssm_input = draw_ssm_input(jax.random.fold_in(jax.random.fold_in(key_list[16], part), 71), part)
    gate_input = gaussian(part_splits[5], (ALL_NEW_ENTRIES, SSM_HEADS * SSM_DIM), 1.0, 5.0, ((0, 4), (1, 4)))
    state_maps = gaussian(part_splits[6], (ALL_NEW_ENTRIES, 2, STATE), 0.3, 1.5, ((0, 4),))
    step_size = draw_step_size(jax.random.fold_in(jax.random.fold_in(key_list[16], part), 71), part)
    decay_log = jnp.clip(jax.random.uniform(key_list[8], (SSM_HEADS,), jnp.float32, -0.5, 0.5) * block_levels(key_list[8], (SSM_HEADS,), ((0, 4),), -0.4, 0.0), -0.5, 0.5)
    skip = draw_skip(jax.random.fold_in(key_list[16], 71), part)
    norm_gain = jnp.clip(1.0 + 0.18 * jax.random.normal(key_list[10], (SSM_HEADS * SSM_DIM,), jnp.float32), 0.1, 1.9)
    hit_owner_keys = jax.random.split(jax.random.fold_in(part_splits[11], 1), REQS * MAX_BLOCKS // (REQ_DEV * MAX_BLOCKS))
    hit_owner_turns = jax.random.permutation(jax.random.fold_in(part_splits[11], 3), REQS * MAX_BLOCKS // (REQ_DEV * MAX_BLOCKS))
    hit_owner = jax.vmap(lambda own, number: deal_out(jax.random.fold_in(part_splits[11], 2), own, number, REQ_DEV * MAX_BLOCKS, N_STORE, 1, SLOTS, 2))(hit_owner_keys, hit_owner_turns).reshape((REQS, MAX_BLOCKS, 1))
    hit_block = set_ends(jax.random.randint(part_splits[12], (REQS, MAX_BLOCKS), 0, POOL), jax.random.fold_in(part_splits[12], 1), 0, POOL - 1).astype(jnp.int32)
    hit_len = ragged_sizes(part_splits[13], REQS, REQS * MAX_BLOCKS * 7 // 8, MAX_BLOCKS, 2).astype(jnp.int32)
    saved_owner_keys = jax.random.split(jax.random.fold_in(part_splits[14], 1), REQS // REQ_DEV)
    saved_owner_turns = jax.random.permutation(jax.random.fold_in(part_splits[14], 3), REQS // REQ_DEV)
    saved_owner = jax.vmap(lambda own, number: deal_out(jax.random.fold_in(part_splits[14], 2), own, number, REQ_DEV, N_STORE, 1, STATE_SLOTS, 1))(saved_owner_keys, saved_owner_turns).reshape((REQS, 1))
    saved_slot = set_ends(jax.random.randint(part_splits[15], (REQS,), 0, SAVED), jax.random.fold_in(part_splits[15], 1), 0, SAVED - 1).astype(jnp.int32)
    return {"queries": queries, "suffix_cache": suffix_cache, "cache_blocks": cache_blocks, "cache_states": cache_states, "ssm_input": ssm_input, "gate_input": gate_input, "state_maps": state_maps, "step_size": step_size, "decay_log": decay_log, "skip": skip, "norm_gain": norm_gain, "hit_owner": hit_owner, "hit_block": hit_block, "hit_len": hit_len, "saved_owner": saved_owner, "saved_slot": saved_slot}


def stretch_scan(inputs, in_maps, out_maps, steps, rates, start_state):
    length, head_count, head_width = inputs.shape
    blocks = length // STRETCH
    highest = lax.Precision.HIGHEST
    input_blocks = inputs.reshape(blocks, STRETCH, head_count, head_width)
    in_blocks = in_maps.reshape(blocks, STRETCH, -1)
    out_blocks = out_maps.reshape(blocks, STRETCH, -1)
    step_blocks = steps.reshape(head_count, blocks, STRETCH).transpose(1, 0, 2)
    causal = jnp.arange(STRETCH)[:, None] >= jnp.arange(STRETCH)[None, :]

    def advance(state, piece_list):
        block_in, map_in, map_out, block_steps = piece_list
        running = jnp.cumsum(block_steps * rates[:, None], axis=1)
        spans = jnp.where(causal[None], running[:, :, None] - running[:, None, :], -jnp.inf)
        intersections = jnp.dot(map_out, map_in.T, preferred_element_type=jnp.float32)
        map_in_wide = map_in.astype(jnp.float32)
        map_out_wide = map_out.astype(jnp.float32)
        mixing = jnp.exp(spans) * intersections[None] * block_steps[:, None, :]
        within = jnp.einsum('hij,jhp->ihp', mixing, block_in, precision=highest)
        carried = jnp.einsum('in,hpn->ihp', map_out_wide, state, precision=highest) * jnp.exp(running).T[:, :, None]
        remaining = (jnp.exp(running[:, -1:] - running) * block_steps).T
        update = jnp.einsum('jhp,jn->hpn', remaining[:, :, None] * block_in, map_in_wide, precision=highest)
        new_state = jnp.exp(running[:, -1])[:, None, None] * state + update
        return (new_state, within + carried)
    last_state, results = lax.scan(advance, start_state, (input_blocks, in_blocks, out_blocks, step_blocks))
    return (results.reshape(length, head_count, head_width), last_state)

def reference(queries, suffix_cache, cache_blocks, cache_states, ssm_input, gate_input, state_maps, step_size, decay_log, skip, norm_gain, hit_owner, hit_block, hit_len, saved_owner, saved_slot):
    group = HEADS // ATTENDED_GROUPS
    scale = HEAD_DIM ** (-0.5)
    prefix_rows = MAX_BLOCKS * BLOCK
    key_count = prefix_rows + REQUEST_NEW
    key_place = jnp.arange(key_count)
    asker_position = jnp.arange(REQUEST_NEW)

    def attend(request):
        first = request * REQUEST_NEW
        query_rows = lax.dynamic_slice_in_dim(queries, first, REQUEST_NEW, 0).astype(jnp.float32)
        query_rows = query_rows.reshape(REQUEST_NEW, ATTENDED_GROUPS, group, HEAD_DIM)
        index = (hit_owner[request, :, 0] * POOL + hit_block[request]).astype(jnp.int32)
        blocks = jnp.take(cache_blocks, index, axis=0)
        prefix = blocks.transpose(1, 0, 2, 3).reshape(2, prefix_rows, -1)
        fresh = lax.dynamic_slice_in_dim(suffix_cache, first, REQUEST_NEW, 0).transpose(1, 0, 2)
        joined = jnp.concatenate([prefix, fresh], axis=1).astype(jnp.float32)
        keys = joined[0].reshape(key_count, ATTENDED_GROUPS, HEAD_DIM)
        values = joined[1].reshape(key_count, ATTENDED_GROUPS, HEAD_DIM)
        scores = jnp.einsum('ikgd,jkd->kgij', query_rows, keys) * scale
        visible = jnp.where(key_place[None, :] < prefix_rows, key_place[None, :] // BLOCK < hit_len[request], key_place[None, :] - prefix_rows <= asker_position[:, None])
        peak = lax.optimization_barrier(jnp.max(jnp.where(visible, scores, -jnp.inf), axis=-1, keepdims=True))
        weights = jnp.exp(jnp.where(visible, scores - peak, -jnp.inf))
        total = lax.optimization_barrier(jnp.sum(weights, axis=-1))
        rounded = lax.optimization_barrier(weights.astype(jnp.bfloat16)).astype(jnp.float32)
        mixed = jnp.einsum('kgij,jkd->ikgd', rounded, values)
        result = mixed / total.transpose(2, 0, 1)[..., None]
        return result.astype(jnp.bfloat16).reshape(REQUEST_NEW, HEADS * HEAD_DIM)
    attn_out = lax.map(attend, jnp.arange(REQS, dtype=jnp.int32)).reshape(ALL_NEW_ENTRIES, HEADS * HEAD_DIM)
    rates = -jnp.exp(decay_log)

    def mamba(request):
        first = request * REQUEST_NEW
        inputs = lax.dynamic_slice_in_dim(ssm_input, first, REQUEST_NEW, 0).astype(jnp.float32)
        inputs = inputs.reshape(REQUEST_NEW, SSM_HEADS, SSM_DIM)
        maps = lax.dynamic_slice_in_dim(state_maps, first, REQUEST_NEW, 0)
        steps = lax.dynamic_slice_in_dim(step_size, first, REQUEST_NEW, 1)
        where_saved = (saved_owner[request, 0] * SAVED + saved_slot[request]).astype(jnp.int32)
        start_state = cache_states[where_saved].astype(jnp.float32).reshape(SSM_HEADS, SSM_DIM, STATE)
        outputs, last_state = stretch_scan(inputs, maps[:, 0], maps[:, 1], steps, rates, start_state)
        outputs = outputs + skip[None, :, None] * inputs
        return (outputs.reshape(REQUEST_NEW, SSM_HEADS * SSM_DIM), last_state.reshape(SSM_HEADS * SSM_DIM, STATE))
    outputs, final_state = lax.map(mamba, jnp.arange(REQS, dtype=jnp.int32))
    mixed = outputs.reshape(ALL_NEW_ENTRIES, SSM_HEADS * SSM_DIM) * jax.nn.silu(gate_input.astype(jnp.float32))
    meansq = lax.optimization_barrier(jnp.mean(mixed * mixed, axis=1))
    ssm_out = (mixed * lax.rsqrt(meansq + 1e-05)[:, None] * norm_gain).astype(jnp.bfloat16)
    return (attn_out, ssm_out, final_state)
```

```python
import functools
import math

import jax
import jax.numpy as jnp
from jax import lax
from jax.experimental import pallas as pl
from jax.experimental.pallas import tpu as pltpu
from jax.sharding import PartitionSpec as P

HEAD_DIM = 128
SSM_DIM = 64
STRETCH = 128
REQUEST_NEW = 512
LOG2E = math.log2(math.e)

NT = (((1,), (1,)), ((), ()))


def scan_kernel(
    slot_ref, x_ref, gate_ref, in_ref, out_ref, step_ref, rate_ref, skip_ref, start_ref,
    mixed_ref, square_ref, final_ref, state,
):
    chunk = pl.program_id(1)
    pairs = x_ref.shape[1] // 128
    f32, bf16 = jnp.float32, jnp.bfloat16

    @pl.when(chunk == 0)
    def _():
        for p in range(pairs):
            cols = slice(p * 128, (p + 1) * 128)
            state[:, cols] = start_ref[0, cols, :].astype(f32).T

    row = lax.broadcasted_iota(jnp.int32, (128, 128), 0)
    lane = lax.broadcasted_iota(jnp.int32, (128, 128), 1)
    steps = step_ref[...]
    log_decay = steps * rate_ref[...]
    upper = (row <= lane).astype(f32)
    lower = (row >= lane).astype(f32)
    highest = lax.Precision.HIGHEST
    run_row = jnp.dot(log_decay, upper, precision=highest, preferred_element_type=f32)
    run_col = lax.dot_general(lower, log_decay, NT, precision=highest, preferred_element_type=f32)
    log_step = jnp.where(steps > 0, jnp.log(steps) * LOG2E, -1e30) - run_row
    weight = jnp.exp2(run_row[:, 127:128] + log_step)

    maps_in = in_ref[...]
    maps_out = out_ref[...]
    gram = lax.dot_general(maps_out, maps_in, NT, preferred_element_type=f32)
    gram = jnp.where(row >= lane, gram, 0.0)
    maps_in_t = maps_in.astype(f32).T
    low = lane < SSM_DIM
    squares = jnp.zeros((128, 128), f32)
    for p in range(pairs):
        cols = slice(p * 128, (p + 1) * 128)
        a, b = 2 * p, 2 * p + 1
        run_a = jnp.broadcast_to(run_col[:, a : a + 1], (128, 128))
        run_b = jnp.broadcast_to(run_col[:, b : b + 1], (128, 128))
        mix_a = (jnp.exp2(run_a + log_step[a : a + 1, :]) * gram).astype(bf16)
        mix_b = (jnp.exp2(run_b + log_step[b : b + 1, :]) * gram).astype(bf16)
        in_a = (maps_in_t * weight[a : a + 1, :]).astype(bf16)
        in_b = (maps_in_t * weight[b : b + 1, :]).astype(bf16)
        x = x_ref[:, cols].astype(f32)
        split = jnp.concatenate(
            [jnp.where(low, x, 0.0).astype(bf16), jnp.where(low, 0.0, x).astype(bf16)], axis=0
        )
        left = jnp.concatenate(
            [jnp.concatenate([mix_a, mix_b], axis=1), jnp.concatenate([in_a, in_b], axis=1)], axis=0
        )
        both = jnp.dot(left, split, preferred_element_type=f32)
        grown = jnp.exp2(jnp.where(low, run_a, run_b))
        old = state[:, cols]
        carried = jnp.dot(maps_out, old.astype(bf16), preferred_element_type=f32) * grown
        y = both[:128] + carried + skip_ref[:, cols] * x
        state[:, cols] = old * grown[127:128, :] + both[128:]
        gate = gate_ref[:, cols].astype(f32)
        mixed = y * gate / (1.0 + jnp.exp(-gate))
        squares = squares + mixed * mixed
        mixed_ref[:, cols] = mixed.astype(bf16)
    square_ref[0] = jnp.sum(squares.T, axis=0, keepdims=True)

    @pl.when(chunk == pl.num_programs(1) - 1)
    def _():
        for p in range(pairs):
            cols = slice(p * 128, (p + 1) * 128)
            final_ref[0, cols, :] = state[:, cols].T


def scan(slots, x, gate, maps_in, maps_out, steps, rates, skip, states):
    rows, channels = x.shape
    heads = steps.shape[0]
    requests = rows // REQUEST_NEW
    chunks = REQUEST_NEW // STRETCH
    wide = pl.BlockSpec((STRETCH, channels), lambda r, c, s: (r * chunks + c, 0))
    maps = pl.BlockSpec((STRETCH, 128), lambda r, c, s: (r * chunks + c, 0))
    return pl.pallas_call(
        scan_kernel,
        grid_spec=pltpu.PrefetchScalarGridSpec(
            num_scalar_prefetch=1,
            grid=(requests, chunks),
            in_specs=[
                wide,
                wide,
                maps,
                maps,
                pl.BlockSpec((heads, STRETCH), lambda r, c, s: (0, r * chunks + c)),
                pl.BlockSpec((heads, 1), lambda r, c, s: (0, 0)),
                pl.BlockSpec((1, channels), lambda r, c, s: (0, 0)),
                pl.BlockSpec((1, channels, 128), lambda r, c, s: (s[r], 0, 0)),
            ],
            out_specs=[
                wide,
                pl.BlockSpec((1, 1, STRETCH), lambda r, c, s: (r * chunks + c, 0, 0)),
                pl.BlockSpec((1, channels, 128), lambda r, c, s: (r, 0, 0)),
            ],
            scratch_shapes=[pltpu.VMEM((128, channels), jnp.float32)],
        ),
        out_shape=[
            jax.ShapeDtypeStruct((rows, channels), jnp.bfloat16),
            jax.ShapeDtypeStruct((rows // STRETCH, 1, STRETCH), jnp.float32),
            jax.ShapeDtypeStruct((requests, channels, 128), jnp.float32),
        ],
        compiler_params=pltpu.CompilerParams(vmem_limit_bytes=32 * 1024 * 1024),
        cost_estimate=pl.CostEstimate(
            flops=30_000_000_000, bytes_accessed=20_000_000, transcendentals=10_000_000
        ),
        name="scan",
    )(slots, x, gate, maps_in, maps_out, steps, rates, skip, states)


def attend_kernel(count, index_ref, length_ref, q_ref, new_k_ref, new_v_ref, *rest):
    blocks, out_ref, keys, values = rest[:count], rest[count], rest[count + 1], rest[count + 2]
    request = pl.program_id(0)
    matched = length_ref[request]
    f32, bf16 = jnp.float32, jnp.bfloat16
    tile = 128
    group = q_ref.shape[1] // HEAD_DIM
    prefix = count * tile
    scale = HEAD_DIM ** (-0.5) * LOG2E

    for j in range(count):
        rows = slice(j * tile, (j + 1) * tile)
        keys[rows, :] = blocks[j][0, 0]

        @pl.when(j < matched)
        def _():
            values[rows, :HEAD_DIM] = blocks[j][0, 1]
            values[rows, HEAD_DIM:] = jnp.ones((tile, HEAD_DIM), bf16)

        @pl.when(j >= matched)
        def _():
            values[rows, :] = jnp.zeros((tile, 2 * HEAD_DIM), bf16)

    keys[prefix:, :] = new_k_ref[...]
    values[prefix:, :HEAD_DIM] = new_v_ref[...]
    values[prefix:, HEAD_DIM:] = jnp.ones(new_v_ref.shape, bf16)

    place = lax.broadcasted_iota(jnp.int32, (group * tile, tile), 0) % tile
    causal = lax.broadcasted_iota(jnp.int32, (group * tile, tile), 1) <= place
    for t in range(q_ref.shape[0] // tile):
        rows = slice(t * tile, (t + 1) * tile)
        q = jnp.concatenate(
            [q_ref[rows, g * HEAD_DIM : (g + 1) * HEAD_DIM] for g in range(group)], axis=0
        )
        seen = prefix + t * tile
        old = lax.dot_general(q, keys[:seen, :], NT, preferred_element_type=f32)
        new = lax.dot_general(q, keys[seen : seen + tile, :], NT, preferred_element_type=f32)
        new = jnp.where(causal, new, -jnp.inf)
        peak = jnp.maximum(
            jnp.max(old, axis=1, keepdims=True), jnp.max(new, axis=1, keepdims=True)
        ) * scale
        weights = jnp.concatenate(
            [jnp.exp2(old * scale - peak).astype(bf16), jnp.exp2(new * scale - peak).astype(bf16)],
            axis=1,
        )
        total = jnp.dot(weights, values[: seen + tile, :], preferred_element_type=f32)
        result = (total[:, :HEAD_DIM] / total[:, HEAD_DIM:]).astype(bf16)
        for g in range(group):
            out_ref[rows, g * HEAD_DIM : (g + 1) * HEAD_DIM] = result[g * tile : (g + 1) * tile]


def attend(index, lengths, queries, new_k, new_v, blocks):
    rows, width = queries.shape
    requests = rows // REQUEST_NEW
    kv_heads = new_k.shape[1] // HEAD_DIM
    group_width = width // kv_heads
    block_rows = blocks.shape[2]
    count = index.shape[0] // requests
    wide = pl.BlockSpec((REQUEST_NEW, group_width), lambda r, h, i, n: (r, h))
    new = pl.BlockSpec((REQUEST_NEW, HEAD_DIM), lambda r, h, i, n: (r, h))

    def stored(j):
        return pl.BlockSpec(
            (1, 2, block_rows, HEAD_DIM), lambda r, h, i, n: (i[r * count + j], 0, 0, h)
        )

    key_rows = count * block_rows + REQUEST_NEW
    return pl.pallas_call(
        functools.partial(attend_kernel, count),
        grid_spec=pltpu.PrefetchScalarGridSpec(
            num_scalar_prefetch=2,
            grid=(requests, kv_heads),
            in_specs=[wide, new, new] + [stored(j) for j in range(count)],
            out_specs=wide,
            scratch_shapes=[
                pltpu.VMEM((key_rows, HEAD_DIM), jnp.bfloat16),
                pltpu.VMEM((key_rows, 2 * HEAD_DIM), jnp.bfloat16),
            ],
        ),
        out_shape=jax.ShapeDtypeStruct((rows, width), jnp.bfloat16),
        compiler_params=pltpu.CompilerParams(vmem_limit_bytes=48 * 1024 * 1024),
        cost_estimate=pl.CostEstimate(
            flops=60_000_000_000, bytes_accessed=20_000_000, transcendentals=25_000_000
        ),
        name="attend",
    )(index, lengths, queries, new_k, new_v, *([blocks] * count))


def body(
    queries,
    suffix_cache,
    cache_blocks,
    cache_states,
    ssm_input,
    gate_input,
    state_maps,
    step_size,
    decay_log,
    skip,
    norm_gain,
    hit_owner,
    hit_block,
    hit_len,
    saved_owner,
    saved_slot,
):
    position = lax.axis_index("store")
    requests = queries.shape[0] // REQUEST_NEW
    max_blocks = hit_block.shape[1]
    pool = cache_blocks.shape[0]
    saved = cache_states.shape[0]

    def mine(array):
        return lax.dynamic_slice_in_dim(array, position * requests, requests, 0)

    slots = mine(saved_owner[:, 0] * saved + saved_slot)
    lengths = mine(hit_len)
    index = mine(hit_owner[:, :, 0] * pool + hit_block)
    alive = jnp.arange(max_blocks)[None, :] < lengths[:, None]
    index = jnp.where(alive, index, index[:, :1]).reshape(-1)

    states = lax.all_gather(cache_states, "store", axis=0, tiled=True)
    blocks = lax.all_gather(cache_blocks, "store", axis=0, tiled=True)

    rates = (-jnp.exp(decay_log) * LOG2E)[:, None]
    skip_wide = jnp.repeat(skip, SSM_DIM)[None, :]
    mixed, squares, final_state = scan(
        slots, ssm_input, gate_input, state_maps[:, 0], state_maps[:, 1], step_size, rates,
        skip_wide, states,
    )
    squares = lax.psum(squares, "tensor").reshape(-1)
    attn_out = attend(index, lengths, queries, suffix_cache[:, 0], suffix_cache[:, 1], blocks)
    channels = ssm_input.shape[1] * lax.axis_size("tensor")
    ssm_out = (
        mixed.astype(jnp.float32) * lax.rsqrt(squares / channels + 1e-05)[:, None] * norm_gain
    ).astype(jnp.bfloat16)
    return (attn_out, ssm_out, final_state)


def solution(mesh):
    in_specs = (
        P(("groups", "store"), "tensor"),
        P(("groups", "store"), None, "tensor"),
        P(("groups", "store"), None, None, "tensor"),
        P(("groups", "store"), "tensor", None),
        P(("groups", "store"), "tensor"),
        P(("groups", "store"), "tensor"),
        P(("groups", "store"), None, None),
        P(("groups", "tensor"), "store"),
        P("tensor"),
        P("tensor"),
        P("tensor"),
        P("groups", None, None),
        P("groups", None),
        P("groups"),
        P("groups", None),
        P("groups"),
    )
    out_specs = (
        P(("groups", "store"), "tensor"),
        P(("groups", "store"), "tensor"),
        P(("groups", "store"), "tensor", None),
    )
    return jax.shard_map(body, mesh=mesh, in_specs=in_specs, out_specs=out_specs, check_vma=False)
```

```python
import functools
import math

import jax
import jax.numpy as jnp
from jax import lax
from jax.experimental import pallas as pl
from jax.experimental.pallas import tpu as pltpu
from jax.sharding import PartitionSpec as P

HEAD_DIM = 128
SSM_DIM = 64
STRETCH = 128
REQUEST_NEW = 512
LOG2E = math.log2(math.e)

NT = (((1,), (1,)), ((), ()))


def scan_kernel(
    stores, owner_ref, slot_ref, x_ref, gate_ref, in_ref, out_ref, step_ref, rate_ref, skip_ref,
    *rest,
):
    pools = rest[:stores]
    mixed_ref, square_ref, final_ref, state, starts, sems = rest[stores:]
    request, chunk = pl.program_id(0), pl.program_id(1)
    requests = pl.num_programs(0)
    position = lax.axis_index("store")
    pairs = x_ref.shape[1] // 128
    f32, bf16 = jnp.float32, jnp.bfloat16

    def fetch(which):
        place = position * requests + which
        relative = owner_ref[place] ^ position
        for k in range(stores):

            @pl.when(relative == k)
            def _():
                pltpu.make_async_copy(
                    pools[k].at[slot_ref[place]], starts.at[which % 2], sems.at[which % 2]
                ).start()

    @pl.when((chunk == 0) & (request == 0))
    def _():
        fetch(request)

    @pl.when(chunk == 0)
    def _():
        now = request % 2
        pltpu.make_async_copy(pools[0].at[0], starts.at[now], sems.at[now]).wait()
        for p in range(pairs):
            cols = slice(p * 128, (p + 1) * 128)
            state[:, cols] = starts[now, cols, :].astype(f32).T

        @pl.when(request + 1 < requests)
        def _():
            fetch(request + 1)

    row = lax.broadcasted_iota(jnp.int32, (128, 128), 0)
    lane = lax.broadcasted_iota(jnp.int32, (128, 128), 1)
    steps = step_ref[...]
    log_decay = steps * rate_ref[...]
    upper = (row <= lane).astype(f32)
    lower = (row >= lane).astype(f32)
    highest = lax.Precision.HIGHEST
    run_row = jnp.dot(log_decay, upper, precision=highest, preferred_element_type=f32)
    run_col = lax.dot_general(lower, log_decay, NT, precision=highest, preferred_element_type=f32)
    log_step = jnp.where(steps > 0, jnp.log(steps) * LOG2E, -1e30) - run_row
    weight = jnp.exp2(run_row[:, 127:128] + log_step)

    maps_in = in_ref[...]
    maps_out = out_ref[...]
    gram = lax.dot_general(maps_out, maps_in, NT, preferred_element_type=f32)
    gram = jnp.where(row >= lane, gram, 0.0)
    maps_in_t = maps_in.astype(f32).T
    low = lane < SSM_DIM
    squares = jnp.zeros((128, 128), f32)
    for p in range(pairs):
        cols = slice(p * 128, (p + 1) * 128)
        a, b = 2 * p, 2 * p + 1
        run_a = jnp.broadcast_to(run_col[:, a : a + 1], (128, 128))
        run_b = jnp.broadcast_to(run_col[:, b : b + 1], (128, 128))
        mix_a = (jnp.exp2(run_a + log_step[a : a + 1, :]) * gram).astype(bf16)
        mix_b = (jnp.exp2(run_b + log_step[b : b + 1, :]) * gram).astype(bf16)
        in_a = (maps_in_t * weight[a : a + 1, :]).astype(bf16)
        in_b = (maps_in_t * weight[b : b + 1, :]).astype(bf16)
        x = x_ref[:, cols].astype(f32)
        split = jnp.concatenate(
            [jnp.where(low, x, 0.0).astype(bf16), jnp.where(low, 0.0, x).astype(bf16)], axis=0
        )
        left = jnp.concatenate(
            [jnp.concatenate([mix_a, mix_b], axis=1), jnp.concatenate([in_a, in_b], axis=1)], axis=0
        )
        both = jnp.dot(left, split, preferred_element_type=f32)
        grown = jnp.exp2(jnp.where(low, run_a, run_b))
        old = state[:, cols]
        carried = jnp.dot(maps_out, old.astype(bf16), preferred_element_type=f32) * grown
        y = both[:128] + carried + skip_ref[:, cols] * x
        state[:, cols] = old * grown[127:128, :] + both[128:]
        gate = gate_ref[:, cols].astype(f32)
        mixed = y * gate / (1.0 + jnp.exp(-gate))
        squares = squares + mixed * mixed
        mixed_ref[:, cols] = mixed.astype(bf16)
    square_ref[0] = jnp.sum(squares.T, axis=0, keepdims=True)

    @pl.when(chunk == pl.num_programs(1) - 1)
    def _():
        for p in range(pairs):
            cols = slice(p * 128, (p + 1) * 128)
            final_ref[0, cols, :] = state[:, cols].T


def scan(owners, slots, x, gate, maps_in, maps_out, steps, rates, skip, pools):
    rows, channels = x.shape
    heads = steps.shape[0]
    requests = rows // REQUEST_NEW
    chunks = REQUEST_NEW // STRETCH
    wide = pl.BlockSpec((STRETCH, channels), lambda r, c, o, s: (r * chunks + c, 0))
    maps = pl.BlockSpec((STRETCH, 128), lambda r, c, o, s: (r * chunks + c, 0))
    return pl.pallas_call(
        functools.partial(scan_kernel, len(pools)),
        grid_spec=pltpu.PrefetchScalarGridSpec(
            num_scalar_prefetch=2,
            grid=(requests, chunks),
            in_specs=[
                wide,
                wide,
                maps,
                maps,
                pl.BlockSpec((heads, STRETCH), lambda r, c, o, s: (0, r * chunks + c)),
                pl.BlockSpec((heads, 1), lambda r, c, o, s: (0, 0)),
                pl.BlockSpec((1, channels), lambda r, c, o, s: (0, 0)),
            ]
            + [pl.BlockSpec(memory_space=pl.ANY)] * len(pools),
            out_specs=[
                wide,
                pl.BlockSpec((1, 1, STRETCH), lambda r, c, o, s: (r * chunks + c, 0, 0)),
                pl.BlockSpec((1, channels, 128), lambda r, c, o, s: (r, 0, 0)),
            ],
            scratch_shapes=[
                pltpu.VMEM((128, channels), jnp.float32),
                pltpu.VMEM((2, channels, 128), jnp.bfloat16),
                pltpu.SemaphoreType.DMA((2,)),
            ],
        ),
        out_shape=[
            jax.ShapeDtypeStruct((rows, channels), jnp.bfloat16),
            jax.ShapeDtypeStruct((rows // STRETCH, 1, STRETCH), jnp.float32),
            jax.ShapeDtypeStruct((requests, channels, 128), jnp.float32),
        ],
        compiler_params=pltpu.CompilerParams(vmem_limit_bytes=56 * 1024 * 1024),
        cost_estimate=pl.CostEstimate(
            flops=30_000_000_000, bytes_accessed=20_000_000, transcendentals=10_000_000
        ),
        name="scan",
    )(owners, slots, x, gate, maps_in, maps_out, steps, rates, skip, *pools)


def attend_kernel(
    stores, count, owner_ref, block_ref, length_ref, q_ref, new_k_ref, new_v_ref, *rest
):
    pools = rest[:stores]
    out_ref, key_slots, value_slots, sems = rest[stores:]
    requests, kv_heads = pl.num_programs(0), pools[0].shape[3] // HEAD_DIM
    request, head = pl.program_id(0), pl.program_id(1)
    step = request * kv_heads + head
    slot = step % 2
    position = lax.axis_index("store")
    matched = length_ref[position * requests + request]
    keys, values = key_slots.at[slot], value_slots.at[slot]
    f32, bf16 = jnp.float32, jnp.bfloat16
    tile = 128
    group = q_ref.shape[1] // HEAD_DIM
    prefix = count * tile
    scale = HEAD_DIM ** (-0.5) * LOG2E

    def fetch(which):
        owner_row = position * requests + which // kv_heads
        columns = pl.ds(pl.multiple_of((which % kv_heads) * HEAD_DIM, HEAD_DIM), HEAD_DIM)
        into = which % 2
        for j in range(count):
            alive = j < length_ref[owner_row]
            entry = owner_row * count + jnp.where(alive, j, 0)
            relative, number = owner_ref[entry] ^ position, block_ref[entry]
            rows = slice(j * tile, (j + 1) * tile)
            for k in range(stores):

                @pl.when(relative == k)
                def _():
                    pltpu.make_async_copy(
                        pools[k].at[number, 0, :, columns],
                        key_slots.at[into, rows, :],
                        sems.at[into, j, 0],
                    ).start()
                    pltpu.make_async_copy(
                        pools[k].at[number, 1, :, columns],
                        value_slots.at[into, rows, :HEAD_DIM],
                        sems.at[into, j, 1],
                    ).start()

    @pl.when(step == 0)
    def _():
        fetch(step)

    @pl.when(step + 1 < requests * kv_heads)
    def _():
        fetch(step + 1)

    for j in range(count):
        rows = slice(j * tile, (j + 1) * tile)
        stored = pools[0].at[0, 0, :, :HEAD_DIM]
        pltpu.make_async_copy(stored, keys.at[rows, :], sems.at[slot, j, 0]).wait()
        pltpu.make_async_copy(stored, values.at[rows, :HEAD_DIM], sems.at[slot, j, 1]).wait()

        @pl.when(j < matched)
        def _():
            values[rows, HEAD_DIM:] = jnp.ones((tile, HEAD_DIM), bf16)

        @pl.when(j >= matched)
        def _():
            values[rows, :] = jnp.zeros((tile, 2 * HEAD_DIM), bf16)

    keys[prefix:, :] = new_k_ref[...]
    values[prefix:, :HEAD_DIM] = new_v_ref[...]
    values[prefix:, HEAD_DIM:] = jnp.ones(new_v_ref.shape, bf16)

    place = lax.broadcasted_iota(jnp.int32, (group * tile, tile), 0) % tile
    causal = lax.broadcasted_iota(jnp.int32, (group * tile, tile), 1) <= place
    for t in range(q_ref.shape[0] // tile):
        rows = slice(t * tile, (t + 1) * tile)
        q = jnp.concatenate(
            [q_ref[rows, g * HEAD_DIM : (g + 1) * HEAD_DIM] for g in range(group)], axis=0
        )
        seen = prefix + t * tile
        old = lax.dot_general(q, keys[:seen, :], NT, preferred_element_type=f32)
        new = lax.dot_general(q, keys[seen : seen + tile, :], NT, preferred_element_type=f32)
        new = jnp.where(causal, new, -jnp.inf)
        peak = jnp.maximum(
            jnp.max(old, axis=1, keepdims=True), jnp.max(new, axis=1, keepdims=True)
        ) * scale
        weights = jnp.concatenate(
            [jnp.exp2(old * scale - peak).astype(bf16), jnp.exp2(new * scale - peak).astype(bf16)],
            axis=1,
        )
        total = jnp.dot(weights, values[: seen + tile, :], preferred_element_type=f32)
        result = (total[:, :HEAD_DIM] / total[:, HEAD_DIM:]).astype(bf16)
        for g in range(group):
            out_ref[rows, g * HEAD_DIM : (g + 1) * HEAD_DIM] = result[g * tile : (g + 1) * tile]


def attend(owners, numbers, lengths, queries, new_k, new_v, pools):
    rows, width = queries.shape
    requests = rows // REQUEST_NEW
    kv_heads = new_k.shape[1] // HEAD_DIM
    group_width = width // kv_heads
    count = owners.shape[0] // lengths.shape[0]
    wide = pl.BlockSpec((REQUEST_NEW, group_width), lambda r, h, o, b, n: (r, h))
    new = pl.BlockSpec((REQUEST_NEW, HEAD_DIM), lambda r, h, o, b, n: (r, h))
    key_rows = count * pools[0].shape[2] + REQUEST_NEW
    return pl.pallas_call(
        functools.partial(attend_kernel, len(pools), count),
        grid_spec=pltpu.PrefetchScalarGridSpec(
            num_scalar_prefetch=3,
            grid=(requests, kv_heads),
            in_specs=[wide, new, new] + [pl.BlockSpec(memory_space=pl.ANY)] * len(pools),
            out_specs=wide,
            scratch_shapes=[
                pltpu.VMEM((2, key_rows, HEAD_DIM), jnp.bfloat16),
                pltpu.VMEM((2, key_rows, 2 * HEAD_DIM), jnp.bfloat16),
                pltpu.SemaphoreType.DMA((2, count, 2)),
            ],
        ),
        out_shape=jax.ShapeDtypeStruct((rows, width), jnp.bfloat16),
        compiler_params=pltpu.CompilerParams(vmem_limit_bytes=56 * 1024 * 1024),
        cost_estimate=pl.CostEstimate(
            flops=60_000_000_000, bytes_accessed=20_000_000, transcendentals=25_000_000
        ),
        name="attend",
    )(owners, numbers, lengths, queries, new_k, new_v, *pools)


def swap(array, bit):
    stores = lax.axis_size("store")
    return lax.ppermute(array, "store", [(i, i ^ bit) for i in range(stores)])


def from_own(array):
    held, bit = {0: array}, 1
    while bit < lax.axis_size("store"):
        held[bit] = array
        bit *= 2
    return {k: swap(array, k) if k else array for k in sorted(held, reverse=True)}


def relayed(held):
    for k in range(1, lax.axis_size("store")):
        if k not in held:
            held[k] = swap(held[k & (k - 1)], k & -k)
    return [held[k] for k in range(lax.axis_size("store"))]


def body(
    queries,
    suffix_cache,
    cache_blocks,
    cache_states,
    ssm_input,
    gate_input,
    state_maps,
    step_size,
    decay_log,
    skip,
    norm_gain,
    hit_owner,
    hit_block,
    hit_len,
    saved_owner,
    saved_slot,
):
    first = from_own(cache_states)
    cache_blocks, first = lax.optimization_barrier((cache_blocks, first))
    states = relayed(first)
    blocks = from_own(cache_blocks)

    rates = (-jnp.exp(decay_log) * LOG2E)[:, None]
    skip_wide = jnp.repeat(skip, SSM_DIM)[None, :]
    mixed, squares, final_state = scan(
        saved_owner.reshape(-1), saved_slot, ssm_input, gate_input, state_maps[:, 0], state_maps[:, 1], step_size, rates,
        skip_wide, states,
    )
    blocks, squares = lax.optimization_barrier((blocks, squares))
    blocks = relayed(blocks)
    parts = lax.axis_size("tensor")
    others = [
        lax.ppermute(squares, "tensor", [(i, (i + k) % parts) for i in range(parts)])
        for k in range(1, parts)
    ]
    attn_out = attend(
        hit_owner.reshape(-1), hit_block.reshape(-1), hit_len, queries, suffix_cache[:, 0],
        suffix_cache[:, 1], blocks,
    )
    squares = sum(others, squares).reshape(-1)
    channels = ssm_input.shape[1] * parts
    ssm_out = (
        mixed.astype(jnp.float32) * lax.rsqrt(squares / channels + 1e-05)[:, None] * norm_gain
    ).astype(jnp.bfloat16)
    return (attn_out, ssm_out, final_state)


def solution(mesh):
    in_specs = (
        P(("groups", "store"), "tensor"),
        P(("groups", "store"), None, "tensor"),
        P(("groups", "store"), None, None, "tensor"),
        P(("groups", "store"), "tensor", None),
        P(("groups", "store"), "tensor"),
        P(("groups", "store"), "tensor"),
        P(("groups", "store"), None, None),
        P(("groups", "tensor"), "store"),
        P("tensor"),
        P("tensor"),
        P("tensor"),
        P("groups", None, None),
        P("groups", None),
        P("groups"),
        P("groups", None),
        P("groups"),
    )
    out_specs = (
        P(("groups", "store"), "tensor"),
        P(("groups", "store"), "tensor"),
        P(("groups", "store"), "tensor", None),
    )
    return jax.shard_map(body, mesh=mesh, in_specs=in_specs, out_specs=out_specs, check_vma=False)
```

```python
import functools
import math

import jax
import jax.numpy as jnp
from jax import lax
from jax.experimental import pallas as pl
from jax.experimental.pallas import tpu as pltpu
from jax.sharding import PartitionSpec as P

HEAD_DIM = 128
SSM_DIM = 64
STRETCH = 128
REQUEST_NEW = 512
LOG2E = math.log2(math.e)

NT = (((1,), (1,)), ((), ()))


def scan_kernel(
    stores, owner_ref, slot_ref, x_ref, gate_ref, in_ref, out_ref, step_ref, rate_ref, skip_ref,
    *rest,
):
    pools = rest[:stores]
    mixed_ref, square_ref, final_ref, state, starts, sems = rest[stores:]
    request, chunk = pl.program_id(0), pl.program_id(1)
    requests = pl.num_programs(0)
    position = lax.axis_index("store")
    pairs = x_ref.shape[1] // 128
    f32, bf16 = jnp.float32, jnp.bfloat16

    def fetch(which):
        place = position * requests + which
        relative = owner_ref[place] ^ position
        for k in range(stores):

            @pl.when(relative == k)
            def _():
                pltpu.make_async_copy(
                    pools[k].at[slot_ref[place]], starts.at[which % 2], sems.at[which % 2]
                ).start()

    @pl.when((chunk == 0) & (request == 0))
    def _():
        fetch(request)

    @pl.when(chunk == 0)
    def _():
        now = request % 2
        pltpu.make_async_copy(pools[0].at[0], starts.at[now], sems.at[now]).wait()
        for p in range(pairs):
            cols = slice(p * 128, (p + 1) * 128)
            state[:, cols] = starts[now, cols, :].astype(f32).T

        @pl.when(request + 1 < requests)
        def _():
            fetch(request + 1)

    row = lax.broadcasted_iota(jnp.int32, (128, 128), 0)
    lane = lax.broadcasted_iota(jnp.int32, (128, 128), 1)
    steps = step_ref[...]
    log_decay = steps * rate_ref[...]
    upper = (row <= lane).astype(f32)
    lower = (row >= lane).astype(f32)
    highest = lax.Precision.HIGHEST
    run_row = jnp.dot(log_decay, upper, precision=highest, preferred_element_type=f32)
    run_col = lax.dot_general(lower, log_decay, NT, precision=highest, preferred_element_type=f32)
    log_step = jnp.where(steps > 0, jnp.log(steps) * LOG2E, -1e30) - run_row
    weight = jnp.exp2(run_row[:, 127:128] + log_step)

    maps_in = in_ref[...]
    maps_out = out_ref[...]
    gram = lax.dot_general(maps_out, maps_in, NT, preferred_element_type=f32)
    gram = jnp.where(row >= lane, gram, 0.0)
    maps_in_t = maps_in.astype(f32).T
    low = lane < SSM_DIM
    squares = jnp.zeros((128, 128), f32)
    for p in range(pairs):
        cols = slice(p * 128, (p + 1) * 128)
        a, b = 2 * p, 2 * p + 1
        run_a = jnp.broadcast_to(run_col[:, a : a + 1], (128, 128))
        run_b = jnp.broadcast_to(run_col[:, b : b + 1], (128, 128))
        mix_a = (jnp.exp2(run_a + log_step[a : a + 1, :]) * gram).astype(bf16)
        mix_b = (jnp.exp2(run_b + log_step[b : b + 1, :]) * gram).astype(bf16)
        in_a = (maps_in_t * weight[a : a + 1, :]).astype(bf16)
        in_b = (maps_in_t * weight[b : b + 1, :]).astype(bf16)
        x = x_ref[:, cols].astype(f32)
        split = jnp.concatenate(
            [jnp.where(low, x, 0.0).astype(bf16), jnp.where(low, 0.0, x).astype(bf16)], axis=0
        )
        left = jnp.concatenate(
            [jnp.concatenate([mix_a, mix_b], axis=1), jnp.concatenate([in_a, in_b], axis=1)], axis=0
        )
        both = jnp.dot(left, split, preferred_element_type=f32)
        grown = jnp.exp2(jnp.where(low, run_a, run_b))
        old = state[:, cols]
        carried = jnp.dot(maps_out, old.astype(bf16), preferred_element_type=f32) * grown
        y = both[:128] + carried + skip_ref[:, cols] * x
        state[:, cols] = old * grown[127:128, :] + both[128:]
        gate = gate_ref[:, cols].astype(f32)
        mixed = y * gate / (1.0 + jnp.exp(-gate))
        squares = squares + mixed * mixed
        mixed_ref[:, cols] = mixed.astype(bf16)
    square_ref[0] = jnp.sum(squares.T, axis=0, keepdims=True)

    @pl.when(chunk == pl.num_programs(1) - 1)
    def _():
        for p in range(pairs):
            cols = slice(p * 128, (p + 1) * 128)
            final_ref[0, cols, :] = state[:, cols].T


def scan(owners, slots, x, gate, maps_in, maps_out, steps, rates, skip, pools):
    rows, channels = x.shape
    heads = steps.shape[0]
    requests = rows // REQUEST_NEW
    chunks = REQUEST_NEW // STRETCH
    wide = pl.BlockSpec((STRETCH, channels), lambda r, c, o, s: (r * chunks + c, 0))
    maps = pl.BlockSpec((STRETCH, 128), lambda r, c, o, s: (r * chunks + c, 0))
    return pl.pallas_call(
        functools.partial(scan_kernel, len(pools)),
        grid_spec=pltpu.PrefetchScalarGridSpec(
            num_scalar_prefetch=2,
            grid=(requests, chunks),
            in_specs=[
                wide,
                wide,
                maps,
                maps,
                pl.BlockSpec((heads, STRETCH), lambda r, c, o, s: (0, r * chunks + c)),
                pl.BlockSpec((heads, 1), lambda r, c, o, s: (0, 0)),
                pl.BlockSpec((1, channels), lambda r, c, o, s: (0, 0)),
            ]
            + [pl.BlockSpec(memory_space=pl.ANY)] * len(pools),
            out_specs=[
                wide,
                pl.BlockSpec((1, 1, STRETCH), lambda r, c, o, s: (r * chunks + c, 0, 0)),
                pl.BlockSpec((1, channels, 128), lambda r, c, o, s: (r, 0, 0)),
            ],
            scratch_shapes=[
                pltpu.VMEM((128, channels), jnp.float32),
                pltpu.VMEM((2, channels, 128), jnp.bfloat16),
                pltpu.SemaphoreType.DMA((2,)),
            ],
        ),
        out_shape=[
            jax.ShapeDtypeStruct((rows, channels), jnp.bfloat16),
            jax.ShapeDtypeStruct((rows // STRETCH, 1, STRETCH), jnp.float32),
            jax.ShapeDtypeStruct((requests, channels, 128), jnp.float32),
        ],
        compiler_params=pltpu.CompilerParams(vmem_limit_bytes=56 * 1024 * 1024),
        cost_estimate=pl.CostEstimate(
            flops=30_000_000_000, bytes_accessed=20_000_000, transcendentals=10_000_000
        ),
        name="scan",
    )(owners, slots, x, gate, maps_in, maps_out, steps, rates, skip, *pools)


def attend_kernel(
    stores, count, owner_ref, block_ref, length_ref, q_ref, new_k_ref, new_v_ref, *rest
):
    pools = rest[:stores]
    out_ref, key_slots, value_slots, sems = rest[-4:]
    requests, request = pl.num_programs(0), pl.program_id(0)
    slot = request % 2
    position = lax.axis_index("store")
    matched = length_ref[position * requests + request]
    keys, values = key_slots.at[slot], value_slots.at[slot]
    f32, bf16 = jnp.float32, jnp.bfloat16
    tile = 128
    group = q_ref.shape[1] // HEAD_DIM
    prefix = count * tile
    scale = HEAD_DIM ** (-0.5) * LOG2E

    def fetch(which):
        owner_row = position * requests + which
        into = which % 2
        for j in range(count):
            alive = j < length_ref[owner_row]
            entry = owner_row * count + jnp.where(alive, j, 0)
            relative, number = owner_ref[entry] ^ position, block_ref[entry]
            rows = slice(j * tile, (j + 1) * tile)
            for k in range(stores):

                @pl.when(relative == k)
                def _():
                    pltpu.make_async_copy(
                        pools[k].at[number, 0],
                        key_slots.at[into, rows, :],
                        sems.at[into, j, 0],
                    ).start()
                    pltpu.make_async_copy(
                        pools[k].at[number, 1],
                        value_slots.at[into, rows, :HEAD_DIM],
                        sems.at[into, j, 1],
                    ).start()

    @pl.when(request == 0)
    def _():
        fetch(request)

    @pl.when(request + 1 < requests)
    def _():
        fetch(request + 1)

    for j in range(count):
        rows = slice(j * tile, (j + 1) * tile)
        stored = pools[0].at[0, 0]
        pltpu.make_async_copy(stored, keys.at[rows, :], sems.at[slot, j, 0]).wait()
        pltpu.make_async_copy(stored, values.at[rows, :HEAD_DIM], sems.at[slot, j, 1]).wait()

        @pl.when(j < matched)
        def _():
            values[rows, HEAD_DIM:] = jnp.ones((tile, HEAD_DIM), bf16)

        @pl.when(j >= matched)
        def _():
            values[rows, :] = jnp.zeros((tile, 2 * HEAD_DIM), bf16)

    keys[prefix:, :] = new_k_ref[...]
    values[prefix:, :HEAD_DIM] = new_v_ref[...]
    values[prefix:, HEAD_DIM:] = jnp.ones(new_v_ref.shape, bf16)

    place = lax.broadcasted_iota(jnp.int32, (group * tile, tile), 0) % tile
    causal = lax.broadcasted_iota(jnp.int32, (group * tile, tile), 1) <= place
    for t in range(q_ref.shape[0] // tile):
        rows = slice(t * tile, (t + 1) * tile)
        q = jnp.concatenate(
            [q_ref[rows, g * HEAD_DIM : (g + 1) * HEAD_DIM] for g in range(group)], axis=0
        )
        seen = prefix + t * tile
        old = lax.dot_general(q, keys[:seen, :], NT, preferred_element_type=f32)
        new = lax.dot_general(q, keys[seen : seen + tile, :], NT, preferred_element_type=f32)
        new = jnp.where(causal, new, -jnp.inf)
        peak = jnp.maximum(
            jnp.max(old, axis=1, keepdims=True), jnp.max(new, axis=1, keepdims=True)
        ) * scale
        weights = jnp.concatenate(
            [jnp.exp2(old * scale - peak).astype(bf16), jnp.exp2(new * scale - peak).astype(bf16)],
            axis=1,
        )
        total = jnp.dot(weights, values[: seen + tile, :], preferred_element_type=f32)
        result = (total[:, :HEAD_DIM] / total[:, HEAD_DIM:]).astype(bf16)
        for g in range(group):
            out_ref[rows, g * HEAD_DIM : (g + 1) * HEAD_DIM] = result[g * tile : (g + 1) * tile]


def attend(head, done, owners, numbers, lengths, queries, new_k, new_v, pools):
    rows, width = queries.shape
    requests = rows // REQUEST_NEW
    kv_heads = new_k.shape[1] // HEAD_DIM
    group_width = width // kv_heads
    count = owners.shape[0] // lengths.shape[0]
    wide = pl.BlockSpec((REQUEST_NEW, group_width), lambda r, o, b, n: (r, head))
    new = pl.BlockSpec((REQUEST_NEW, HEAD_DIM), lambda r, o, b, n: (r, head))
    key_rows = count * pools[0].shape[2] + REQUEST_NEW
    return pl.pallas_call(
        functools.partial(attend_kernel, len(pools), count),
        grid_spec=pltpu.PrefetchScalarGridSpec(
            num_scalar_prefetch=3,
            grid=(requests,),
            in_specs=[wide, new, new] + [pl.BlockSpec(memory_space=pl.ANY)] * (len(pools) + len(done)),
            out_specs=wide,
            scratch_shapes=[
                pltpu.VMEM((2, key_rows, HEAD_DIM), jnp.bfloat16),
                pltpu.VMEM((2, key_rows, 2 * HEAD_DIM), jnp.bfloat16),
                pltpu.SemaphoreType.DMA((2, count, 2)),
            ],
        ),
        out_shape=jax.ShapeDtypeStruct((rows, width), jnp.bfloat16),
        compiler_params=pltpu.CompilerParams(vmem_limit_bytes=56 * 1024 * 1024),
        cost_estimate=pl.CostEstimate(
            flops=30_000_000_000, bytes_accessed=20_000_000, transcendentals=12_000_000
        ),
        input_output_aliases={6 + len(pools): 0} if done else {},
        name="attend",
    )(owners, numbers, lengths, queries, new_k, new_v, *pools, *done)


def swap(array, bit):
    stores = lax.axis_size("store")
    return lax.ppermute(array, "store", [(i, i ^ bit) for i in range(stores)])


def from_own(array):
    held, bit = {0: array}, 1
    while bit < lax.axis_size("store"):
        held[bit] = array
        bit *= 2
    return {k: swap(array, k) if k else array for k in sorted(held, reverse=True)}


def relayed(held):
    for k in range(1, lax.axis_size("store")):
        if k not in held:
            held[k] = swap(held[k & (k - 1)], k & -k)
    return [held[k] for k in range(lax.axis_size("store"))]


def body(
    queries,
    suffix_cache,
    cache_blocks,
    cache_states,
    ssm_input,
    gate_input,
    state_maps,
    step_size,
    decay_log,
    skip,
    norm_gain,
    hit_owner,
    hit_block,
    hit_len,
    saved_owner,
    saved_slot,
):
    kv_heads = cache_blocks.shape[3] // HEAD_DIM
    first = from_own(cache_states)
    pieces = [cache_blocks[..., h * HEAD_DIM : (h + 1) * HEAD_DIM] for h in range(kv_heads)]
    new_k, new_v = suffix_cache[:, 0], suffix_cache[:, 1]
    maps_in, maps_out = state_maps[:, 0], state_maps[:, 1]
    rates = (-jnp.exp(decay_log) * LOG2E)[:, None]
    skip_wide = jnp.repeat(skip, SSM_DIM)[None, :]
    hits = hit_owner.reshape(-1), hit_block.reshape(-1)
    first, pieces, new_k, new_v, maps_in, maps_out, rates, skip_wide, hits = (
        lax.optimization_barrier(
            (first, pieces, new_k, new_v, maps_in, maps_out, rates, skip_wide, hits)
        )
    )
    states = relayed(first)
    blocks = from_own(pieces[0])

    mixed, squares, final_state = scan(
        saved_owner.reshape(-1), saved_slot, ssm_input, gate_input, maps_in, maps_out, step_size,
        rates, skip_wide, states,
    )
    blocks, squares, pieces = lax.optimization_barrier((blocks, squares, pieces))
    parts = lax.axis_size("tensor")
    others = [
        lax.ppermute(squares, "tensor", [(i, (i + k) % parts) for i in range(parts)])
        for k in range(1, parts)
    ]
    done = []
    for h in range(kv_heads):
        later = from_own(pieces[h + 1]) if h + 1 < kv_heads else None
        done = [
            attend(h, done, *hits, hit_len, queries, new_k, new_v, relayed(blocks))
        ]
        if later is not None:
            blocks, done = lax.optimization_barrier((later, done))
    attn_out = done[0]
    squares = sum(others, squares).reshape(-1)
    channels = ssm_input.shape[1] * parts
    ssm_out = (
        mixed.astype(jnp.float32) * lax.rsqrt(squares / channels + 1e-05)[:, None] * norm_gain
    ).astype(jnp.bfloat16)
    return (attn_out, ssm_out, final_state)


def solution(mesh):
    in_specs = (
        P(("groups", "store"), "tensor"),
        P(("groups", "store"), None, "tensor"),
        P(("groups", "store"), None, None, "tensor"),
        P(("groups", "store"), "tensor", None),
        P(("groups", "store"), "tensor"),
        P(("groups", "store"), "tensor"),
        P(("groups", "store"), None, None),
        P(("groups", "tensor"), "store"),
        P("tensor"),
        P("tensor"),
        P("tensor"),
        P("groups", None, None),
        P("groups", None),
        P("groups"),
        P("groups", None),
        P("groups"),
    )
    out_specs = (
        P(("groups", "store"), "tensor"),
        P(("groups", "store"), "tensor"),
        P(("groups", "store"), "tensor", None),
    )
    return jax.shard_map(body, mesh=mesh, in_specs=in_specs, out_specs=out_specs, check_vma=False)
```
